32 devices in a mesh: views: 2 (over y), tiles: 16 (over z, x, core).
Axes of the slice: x: 2, y: 2, z: 4, core: 2. Of those that a mesh axis runs over, the one named last changes fastest.
Arguments:
- linear_point: float32 [59, 8192], P(None, 'tiles'), may hold values from -6 to 6
- right_side: float32 [59, 8192], P(None, 'tiles'), may hold values from -75 to 75
- damping: float32 [59, 8192], P(None, 'tiles'), may hold values from 0.2 to 2
- projection: float32 [2, 59, 16], P('views'), may hold values from -0.75 to 0.75
- pixel_basis: float32 [2, 16, 12, 128], P('views', 'tiles'), may hold values from -1.8 to 1.8
- pixel_weight: float32 [2, 16, 128], P('views', 'tiles'), may hold values from 50 to 500
- depth_order: int32 [2, 16, 512], P('views', 'tiles'), may hold values from 0 to 511, each once within a row
- tile_dest: int32 [2, 1024, 1], P('views', 'tiles'), may hold values from 0 to 15; in each aligned block of 64 rows (0 to 63, 64 to 127, ..., all dimensions but the last counted through in order) at most 4 rows name the same one
- block_depth: int32 [2, 1024], P('views', 'tiles'), may hold values from 0 to 1023, each once within a row
Outputs:
- solution: float32 [59, 8192], P(None, 'tiles')
- residual: float32 [59, 8192], P(None, 'tiles')
The draws below stay inside these ranges and needn't reach their ends.
Inputs may be any that keep to these rules, and one draw needn't show every extreme that they name: `tile_dest`: each block of one owner in one view names one tile; no tile is named by more than 4 blocks of one owner in one view, a bound that the blocks of some owner reach; every tile is named by some block of every view. `depth_order`: for each view and owner, a permutation of the owner's local Gaussian numbers. `block_depth`: for each view, a permutation of the block numbers.
All inputs are finite; a program needn't handle non-finite values.
Results may differ from the reference program's by a relative error of at most 0.007.
Values sent between devices are 32-bit elements; how exact they have to be, the bound alone decides.
A program may use at most 64 MiB of HBM per device.

```python
import math
import jax
import jax.numpy as jnp
import numpy as np
from jax import lax

PARAMS = 59
FEAT = 16
PIX = 128
ROWS = 8
ITERS = 2
BLK_DEV = 64
G_DEV = 512
VIEWS = 2
TILE_COUNT = 16
CAP = 4
GAUSS = 8192
BLOCKS = 1024


def draw_right_side(key, part):
    key = jax.random.fold_in(key, 11)
    key_base, key_cols, key_rows = jax.random.split(key, 3)
    base = jnp.clip(jax.random.normal(key_base, (PARAMS, GAUSS), jnp.float32), -4.0, 4.0)
    col_scale = jnp.exp(jax.random.uniform(key_cols, (1, GAUSS), jnp.float32) * math.log(10.0))
    row_scale = jnp.exp(jax.random.uniform(key_rows, (PARAMS, 1), jnp.float32) * math.log(3.0))
    trend = jnp.exp(jnp.arange(GAUSS, dtype=jnp.float32)[None, :] * (math.log(3.0) / GAUSS))
    return (base * col_scale * row_scale * trend / 6.0).astype(jnp.float32)


def block_levels(stream_key, dims, shards, least, largest):
    def one(position, blocks):
        steps = jax.random.uniform(jax.random.fold_in(jax.random.fold_in(stream_key, 6), position), (blocks,), jnp.float32, least / len(shards), largest / len(shards))
        return jnp.repeat(jnp.exp(steps), dims[position] // blocks).reshape((-1,) + (1,) * (len(dims) - position - 1))

    loudness = one(*shards[0])
    for cut in shards[1:]:
        loudness = loudness * one(*cut)
    return loudness


def routed_block(key, own, number, rows, number_of, top, limit, slope):
    order = jax.random.permutation(key, number_of)
    packed, ordinary = shares(number_of, rows * top, limit, slope, True), shares(number_of, rows * top, limit, slope, False)
    places = jnp.arange(number_of)

    def named(lengths, rotation):
        used = int((lengths > 0).sum())
        fixed = max(1, used // 4)
        passed = fixed + (places - fixed + rotation * (used - fixed)) % max(1, number_of - fixed)
        return jnp.zeros((number_of,), jnp.int32).at[order[jnp.where(places < fixed, places, passed)]].set(jnp.asarray(lengths, jnp.int32))

    lengths = jnp.where(number % 4 == 0, named(packed, number // 4), named(ordinary, number - number // 4 - 1))
    mixed = jax.random.permutation(jax.random.fold_in(own, 3), number_of)
    giver, taker = mixed[0:number_of // 2 * 2:2], mixed[1:number_of // 2 * 2:2]
    room = jnp.minimum(lengths[giver] - 1, limit - lengths[taker]) // 2
    room = jnp.where((giver == order[0]) | (taker == order[0]) | (lengths[taker] == 0), 0, jnp.maximum(room, 0))
    passed = jax.random.randint(jax.random.fold_in(own, 4), (number_of // 2,), 0, 1 << 20) % (room + 1)
    lengths = lengths.at[giver].add(-passed).at[taker].add(passed)
    items = jnp.searchsorted(jnp.cumsum(lengths), jnp.arange(rows * top), side="right").astype(jnp.int32)
    table = items.reshape(top, rows).T
    table = table[jax.random.permutation(jax.random.fold_in(own, 1), rows)]
    rotation = jax.random.randint(jax.random.fold_in(own, 2), (rows, 1), 0, top)
    return jnp.take_along_axis(table, (jnp.arange(top)[None, :] + rotation) % top, axis=1)


def shares(count, total, reach, skew, full):
    loads = [(1 << 20) // math.isqrt(grade ** skew) + 1 for grade in range(1, count + 1)]
    largest = reach if full else min(reach, max(-(-total // count), total * loads[0] // sum(loads)))
    least = 1 if total - largest >= count - 1 else 0
    counts, rest = [largest] + [least] * (count - 1), total - largest - least * (count - 1)
    while rest > 0:
        free = [i for i in range(1, count) if counts[i] < largest] or [i for i in range(1, count) if counts[i] < reach]
        mass, budget = sum([loads[i] for i in free]), rest
        for i in free:
            more = min(reach - counts[i], max(1, budget * loads[i] // mass), rest)
            counts[i] = counts[i] + more
            rest = rest - more
    return np.array(counts)


def bell_draw(own_key, extent, scale, reach, shards=(), kind=jnp.bfloat16):
    level = block_levels(own_key, extent, shards, -0.22, 0.18) if shards else 1.0
    result = jax.random.normal(own_key, extent, jnp.float32) * scale * level
    return jnp.minimum(jnp.maximum(result, -reach), reach).astype(kind)


def setup_inputs(seed: int = 0) -> dict:
    key_of = jax.random.split(jax.random.key(seed), 10)
    linear_point = bell_draw(key_of[0], (PARAMS, GAUSS), 1.0, 6.0, ((1, 16),), jnp.float32)
    right_side = draw_right_side(jax.random.fold_in(key_of[9], 71), 0)
    damping = jnp.clip(jnp.exp(math.log(2.0) - 2.3025851 * jax.random.uniform(key_of[2], (PARAMS, GAUSS), jnp.float32) ** block_levels(key_of[2], (PARAMS, GAUSS), ((1, 16),), -0.2, 0.2)), 0.2, 2.0)
    projection = bell_draw(key_of[3], (VIEWS, PARAMS, FEAT), PARAMS ** -0.5, 0.75, ((0, 2),), jnp.float32)
    pixel_basis = bell_draw(key_of[4], (VIEWS, TILE_COUNT, FEAT - 4, PIX), 0.3, 1.8, ((0, 2), (1, 16)), jnp.float32)
    pixel_weight = jnp.clip(jnp.exp(math.log(500.0) - 2.3025851 * jax.random.uniform(key_of[5], (VIEWS, TILE_COUNT, PIX), jnp.float32) ** block_levels(key_of[5], (VIEWS, TILE_COUNT, PIX), ((0, 2), (1, 16)), -0.2, 0.2)), 50.0, 500.0)
    depth_order = jax.vmap(lambda own: jax.random.permutation(own, G_DEV))(jax.random.split(key_of[6], VIEWS * TILE_COUNT)).reshape((VIEWS, TILE_COUNT, G_DEV)).astype(jnp.int32)
    tile_dest_keys = jax.random.split(jax.random.fold_in(key_of[7], 1), VIEWS * BLOCKS // BLK_DEV)
    tile_dest_turns = jax.random.permutation(jax.random.fold_in(key_of[7], 3), VIEWS * BLOCKS // BLK_DEV)
    tile_dest = jax.vmap(lambda own, number: routed_block(jax.random.fold_in(key_of[7], 2), own, number, BLK_DEV, TILE_COUNT, 1, CAP, 1))(tile_dest_keys, tile_dest_turns).reshape((VIEWS, BLOCKS, 1))
    block_depth = jax.vmap(lambda own: jax.random.permutation(own, BLOCKS))(jax.random.split(key_of[8], VIEWS)).reshape((VIEWS, BLOCKS)).astype(jnp.int32)
    return {"linear_point": linear_point, "right_side": right_side, "damping": damping, "projection": projection, "pixel_basis": pixel_basis, "pixel_weight": pixel_weight, "depth_order": depth_order, "tile_dest": tile_dest, "block_depth": block_depth}


PRECISE = lax.Precision.HIGHEST
OFFSET = 6.0

def view_images(params, view_proj, view_basis, view_order, view_dest, view_depth):
    owners = jnp.arange(TILE_COUNT, dtype=jnp.int32)[:, None] * G_DEV
    index = (owners + view_order).reshape(-1).astype(jnp.int32)
    picked = jnp.take(params, index, axis=1).reshape(PARAMS, BLOCKS, ROWS)
    blocks = jnp.einsum('kf,kbr->bfr', view_proj, picked, precision=PRECISE)
    basis_rows = jnp.take(view_basis, view_dest, axis=0)
    logits = blocks[:, 0, :, None] - OFFSET + jnp.einsum('bkr,bkp->brp', blocks[:, 4:, :], basis_rows, precision=PRECISE)
    alphas = jax.nn.sigmoid(logits)
    log_clear = -jax.nn.softplus(logits)
    before = jnp.cumsum(log_clear, axis=1) - log_clear
    colors = jnp.einsum('bcr,brp->bcp', blocks[:, 1:4, :], alphas * jnp.exp(before), precision=PRECISE)
    through = lax.optimization_barrier(jnp.sum(log_clear, axis=1))
    shared = view_dest[None, :] == view_dest[:, None]
    earlier = view_depth[None, :] < view_depth[:, None]
    ahead = jnp.dot((shared & earlier).astype(jnp.float32), through, precision=PRECISE)
    weighted = jnp.exp(ahead)[:, None, :] * colors
    return jax.ops.segment_sum(weighted, view_dest, TILE_COUNT)

def normal_views(direction, linear_point, projection, pixel_basis, pixel_weight, depth_order, tile_dest, block_depth):

    def one_view(view_index):

        def render(params):
            return view_images(params, projection[view_index], pixel_basis[view_index], depth_order[view_index], tile_dest[view_index, :, 0], block_depth[view_index])
        tangent = jax.jvp(render, (linear_point,), (direction,))[1]
        unused_out, pull = jax.vjp(render, linear_point)
        return pull(tangent * pixel_weight[view_index][:, None, :])[0]
    terms = lax.map(one_view, jnp.arange(VIEWS, dtype=jnp.int32))
    return lax.optimization_barrier(jnp.sum(terms, axis=0))

def reference(linear_point, right_side, damping, projection, pixel_basis, pixel_weight, depth_order, tile_dest, block_depth):
    solution = jnp.zeros_like(right_side)
    residual = right_side
    direction = right_side
    norm_now = jnp.sum(residual * residual)
    for iteration in range(ITERS):
        product = normal_views(direction, linear_point, projection, pixel_basis, pixel_weight, depth_order, tile_dest, block_depth) + damping * direction
        step_size = norm_now / jnp.sum(direction * product)
        solution = solution + step_size * direction
        residual = residual - step_size * product
        norm_next = jnp.sum(residual * residual)
        direction = residual + norm_next / norm_now * direction
        norm_now = norm_next
    return (solution, residual)
```

```python
import functools

import jax
import jax.numpy as jnp
from jax import lax
from jax.experimental import pallas as pl
from jax.experimental.pallas import tpu as pltpu
from jax.sharding import PartitionSpec as P

MESH = pl.DeviceIdType.MESH
F32 = jnp.float32
BF16 = jnp.bfloat16
FEATS = 16
OFFSET = 6.0


def dot16(a, b, dims=((1,), (0,))):
    return lax.dot_general(a, b, (dims, ((), ())), preferred_element_type=F32)


def split(x):
    high = x.astype(BF16)
    return high, (x - high.astype(F32)).astype(BF16)


def stacked(x):
    return jnp.concatenate(split(x), axis=0)


def halves_sum(x):
    rows = x.shape[0] // 2
    return x[:rows] + x[rows:]


def pick(x, onehot, dims=((1,), (0,))):
    return halves_sum(dot16(stacked(x), onehot, dims))


def pick_left(twice, x):
    return dot16(twice, stacked(x))


def small_dot(a, b):
    high, low = split(b)
    left = stacked(a)
    return halves_sum(dot16(left, high)) + dot16(left[: a.shape[0]], low)


def wide_dot(a, pair):
    return halves_sum_wide(dot16(stacked(a), pair))


def halves_sum_wide(x):
    rows, lanes = x.shape[0] // 2, x.shape[1] // 2
    return x[:rows, :lanes] + x[rows:, :lanes] + x[:rows, lanes:]


def paired(x):
    return jnp.concatenate(split(x), axis=1)


def wide_dot_t(a, pair):
    high, low = split(a)
    left = jnp.concatenate(
        [
            jnp.concatenate([high, high], axis=1),
            jnp.concatenate([low, jnp.zeros_like(low)], axis=1),
        ],
        axis=0,
    )
    return halves_sum(dot16(left, pair, ((1,), (1,))))


def three_a(x):
    high, low = split(x)
    return jnp.concatenate([high, high, low], axis=0)


def three_b(x):
    high, low = split(x)
    return jnp.concatenate([high, low, high], axis=0)


def iota(shape, axis):
    return lax.broadcasted_iota(jnp.int32, shape, axis)


def total(x):
    return jnp.sum(jnp.sum(x, axis=0, keepdims=True), axis=1, keepdims=True)


def swap_blocks(x, width):
    groups = 128 // width
    depth = FEATS // groups
    rows, lanes = iota(x.shape, 0), iota(x.shape, 1)
    bit = 1
    while bit < groups:
        up, over = depth * bit, width * bit
        row_bit = (rows // up) % 2
        lane_bit = (lanes // over) % 2
        down = pltpu.roll(pltpu.roll(x, FEATS - up, 0), over, 1)
        back = pltpu.roll(pltpu.roll(x, up, 0), 128 - over, 1)
        x = jnp.where(row_bit == lane_bit, x, jnp.where(lane_bit == 1, down, back))
        bit *= 2
    return x


def kernel(
    views,
    tiles,
    *refs,
):
    my_view = lax.axis_index("views")
    me = lax.axis_index("tiles")
    flat = my_view * tiles + me
    everyone = views * tiles
    inputs, refs = refs[:9], refs[9:]
    sol_ref, res_ref, onehot, xbuf = refs[:4]
    f1_send, f1_recv, b1_send, b1_recv, f2_send, f2_recv, b2_send, b2_recv = refs[4:12]
    held, (send_sem, recv_sem, in_sem) = refs[12:21], refs[21:]
    lp_ref, rs_ref, dm_ref, proj_ref, basis_ref, weight_ref, order_ref, dest_ref, depth_ref = held
    fetches = [
        pltpu.make_async_copy(inputs[i], held[i], in_sem.at[i]) for i in range(9)
    ]
    for i in (6, 7, 8, 3, 1, 0, 2, 4, 5):
        fetches[i].start()
    count = dest_ref.shape[1]
    gauss = order_ref.shape[1]
    params = rs_ref.shape[0]
    per = gauss // count
    capacity = max(2, count // tiles)
    width = per * capacity
    places = tiles * width
    blocks = places // 128
    groups = 128 // width
    depth = FEATS // groups

    barrier = pltpu.get_barrier_semaphore()

    def greet(k, carry):
        other = lax.rem(flat + k, everyone)
        pl.semaphore_signal(
            barrier, inc=1, device_id=(other // tiles, lax.rem(other, tiles)), device_id_type=MESH
        )
        return carry

    lax.fori_loop(1, everyone, greet, 0)

    eye = iota((count, count), 0) == iota((count, count), 1)
    for i in (6, 7, 8):
        fetches[i].wait()
    dest_row = dest_ref[...].astype(F32)
    dest = jnp.sum(jnp.where(eye, dest_row, 0.0), axis=1, keepdims=True)
    earlier = iota((count, count), 1) < iota((count, count), 0)
    position = jnp.sum(
        jnp.where((dest_row == dest) & earlier, 1.0, 0.0), axis=1, keepdims=True
    )
    slot = dest * float(capacity) + position
    mark = jnp.sum(jnp.where(eye, depth_ref[...].astype(F32), 0.0), axis=1, keepdims=True) + 1.0
    order = order_ref[...]
    own = iota((count, gauss), 1) // per == iota((count, gauss), 0)
    high = jnp.where(own, (order // 256).astype(F32), 0.0)
    low = jnp.where(own, (order % 256).astype(F32), 0.0)
    spread = (
        iota((gauss, 128), 0) % per == (iota((gauss, 128), 1) % width) // capacity
    ).astype(F32).astype(BF16)
    listed = dot16(jnp.concatenate([high, low], axis=0).astype(BF16), spread)
    listed = listed[:count] * 256.0 + listed[count:] + 1.0
    ids, marks = [], []
    for k in range(blocks):
        lane = iota((count, 128), 1) + k * 128
        wanted = (lane // width) * capacity + lane % capacity
        here = slot == wanted.astype(F32)
        ids.append(jnp.sum(jnp.where(here, listed, 0.0), axis=0, keepdims=True) - 1.0)
        marks.append(jnp.sum(jnp.where(here, mark, 0.0), axis=0, keepdims=True))

    def place_matrix(rows):
        numbers = iota((gauss, 128), 0).astype(F32)
        return jnp.concatenate(
            [(numbers == row).astype(F32).astype(BF16) for row in rows], axis=1
        )

    mine = place_matrix(ids)
    onehot[my_view] = mine
    for i in (3, 1, 0, 2, 4, 5):
        fetches[i].wait()
    proj = proj_ref[...]
    xbuf[my_view, 0:FEATS, 0:params] = proj
    for k in range(blocks):
        xbuf[my_view, FEATS + k : FEATS + 1 + k, :] = ids[k]

    right = rs_ref[...]
    damp = dm_ref[...]
    u_both = jnp.concatenate(
        [small_dot(proj, lp_ref[...]), small_dot(proj, right)], axis=0
    )
    u_both = pick(u_both, mine)
    damped = damp * right
    lane = iota((1, 128), 1)

    def put(buf, start, parts):
        for k in range(blocks):
            for row in range(FEATS):
                buf[k * groups + row // depth, start + row % depth] = parts[k][row : row + 1]

    def swapped(u):
        return [swap_blocks(u[:, k * 128 : k * 128 + 128], width) for k in range(blocks)]

    put(f1_send, 0, swapped(u_both[:FEATS]))
    put(f1_send, depth, swapped(u_both[FEATS:]))
    sums = jnp.where(lane == width, total(right * right), 0.0) + jnp.where(
        lane == width + 1, total(damped * right), 0.0
    )
    top = iota((FEATS, 128), 0) == 0
    for k in range(blocks):
        ranks = swap_blocks(jnp.where(top, marks[k], 0.0), width)
        for j in range(groups):
            f1_send[k * groups + j, 2 * depth] = ranks[j * depth : j * depth + 1] + sums

    pl.semaphore_wait(barrier, everyone - 1)

    def send(src, dst, view, tile, sem):
        return pltpu.make_async_remote_copy(
            src_ref=src,
            dst_ref=dst,
            send_sem=send_sem.at[sem],
            recv_sem=recv_sem.at[sem],
            device_id=(view, tile),
            device_id_type=MESH,
        )

    def to_tiles(src, dst, sem):
        def step(k, carry):
            other = lax.rem(me + k, tiles)
            send(src.at[other], dst.at[me], my_view, other, sem).start()
            return carry

        lax.fori_loop(1, tiles, step, 0)
        dst[me] = src[me]

    def to_owners(src, dst, sem):
        def step(k, carry):
            other = lax.rem(flat + k, everyone)
            tile = lax.rem(other, tiles)
            send(src.at[tile], dst.at[flat], other // tiles, tile, sem).start()
            return carry

        lax.fori_loop(1, everyone, step, 0)
        dst[flat] = src[me]

    def landed(dst, number, sem):
        whole = dst.at[pl.ds(0, number)]
        send(whole, whole, my_view, me, sem).wait_recv()

    def left(src, number, sem):
        whole = src.at[pl.ds(0, number)]
        send(whole, whole, my_view, me, sem).wait_send()

    to_tiles(f1_send, f1_recv, 1)
    for k in range(1, views):
        send(xbuf.at[my_view], xbuf.at[my_view], lax.rem(my_view + k, views), me, 0).start()

    basis = jnp.concatenate(
        [jnp.ones((1, 128), F32), jnp.zeros((3, 128), F32)]
        + [basis_ref[i] for i in range(FEATS - 4)],
        axis=0,
    )
    basis3 = three_b(basis)
    weight = weight_ref[...]
    color_row = (iota((FEATS, 128), 0) >= 1) & (iota((FEATS, 128), 0) <= 3)

    landed(f1_recv, tiles - 1, 1)

    def gathered(buf, first, start):
        out = []
        for k in range(blocks):
            rows = [
                buf[first + k * groups + row // depth, start + row % depth] for row in range(FEATS)
            ]
            out.append(swap_blocks(jnp.concatenate(rows, axis=0), width))
        return out

    def turned(parts):
        return jnp.concatenate([part.T for part in parts], axis=0)

    def turned3(parts):
        return turned([three_a(part).astype(F32) for part in parts]).astype(BF16)

    primal_parts = gathered(f1_recv, 0, 0)
    u0 = jnp.concatenate(primal_parts, axis=1)
    u0_t = turned3(primal_parts)
    ranks = []
    for k in range(blocks):
        rows = []
        for j in range(groups):
            row = f1_recv[k * groups + j, 2 * depth]
            rows.append(jnp.where(lane < width, row, 0.0))
            rows.append(jnp.zeros((depth - 1, 128), F32))
        ranks.append(swap_blocks(jnp.concatenate(rows, axis=0), width))
    marks_t = turned(ranks)[:, 0:1]

    def lanes_total(buf, row, number):
        out = buf[0, row]
        for t in range(1, number):
            out = out + buf[t, row]
        return out

    sums = lanes_total(f1_recv, 2 * depth, tiles)
    rr, rdr = sums[:, width : width + 1], sums[:, width + 1 : width + 2]

    halves = 8 // capacity
    steps = width // 8
    small = tiles * 8
    sub = iota((tiles * steps, 8, 128), 1)

    def scan(x):
        x = x.reshape(tiles * steps, 8, 128)
        through = inner = x
        step = 1
        while step < halves:
            shift = step * capacity
            inner = inner + jnp.where(sub >= shift, pltpu.roll(inner, shift, 1), 0.0)
            through = through + pltpu.roll(through, shift, 1)
            step *= 2
        before = inner - x
        through = through.reshape(tiles, steps, 8, 128)
        before = before.reshape(tiles, steps, 8, 128)
        run = jnp.zeros((tiles, 8, 128), F32)
        out = []
        for i in range(steps):
            out.append(before[:, i] + run)
            run = run + through[:, i]
        return jnp.stack(out, axis=1), run

    def wide(x):
        return x.reshape(tiles, 1, 8, 128)

    def full(x):
        return x.reshape(tiles, steps, 8, 128)

    mark_col = marks_t.reshape(tiles, width, 1)[:, 0:8, :].reshape(small, 1)
    square = (small, small)
    mark_row = jnp.sum(
        jnp.where(iota(square, 0) == iota(square, 1), mark_col, 0.0), axis=0, keepdims=True
    )
    first = (iota(square, 1) % 8) < capacity
    ahead = (first & (mark_row < mark_col) & (mark_row > 0.0)).astype(F32).astype(BF16)
    behind = (first & (mark_row > mark_col)).astype(F32).astype(BF16)
    ahead = jnp.concatenate([ahead, ahead], axis=1)
    behind = jnp.concatenate([behind, behind], axis=1)

    z = dot16(u0_t, basis3) - OFFSET
    filled = marks_t > 0.0
    tail = jnp.exp(-jnp.abs(z))
    alpha = jnp.where(filled, jnp.where(z >= 0.0, 1.0, tail) / (1.0 + tail), 0.0)
    clear = jnp.where(filled, -(jnp.maximum(z, 0.0) + jnp.log1p(tail)), 0.0)
    before, through = scan(clear)
    before = before + wide(pick_left(ahead, through.reshape(small, 128)))
    visible = full(alpha) * jnp.exp(before)
    visible_pair = paired(visible.reshape(places, 128))
    alpha = full(alpha)
    rest = 1.0 - alpha

    def image_tangent(parts):
        du = jnp.concatenate(parts, axis=1)
        dz = full(dot16(turned3(parts), basis3))
        before, through = scan(-alpha * dz)
        before = before + wide(pick_left(ahead, through.reshape(small, 128)))
        moved = visible * (rest * dz + before)
        return wide_dot(du, visible_pair) + wide_dot(u0, paired(moved.reshape(places, 128)))

    def cotangent(image, buf):
        image = jnp.where(color_row, image, 0.0)
        pull = image * weight
        energy = jnp.broadcast_to(total(pull * image), (1, 128))
        h = full(dot16(u0_t, three_b(pull))) * visible
        before, through = scan(h)
        later = through + pick_left(behind, through.reshape(small, 128)).reshape(tiles, 8, 128)
        z_bar = h * rest - alpha * (wide(later) - before - h)
        u_bar = wide_dot_t(basis, paired(z_bar.reshape(places, 128))) + wide_dot_t(
            pull, visible_pair
        )
        put(buf, 0, swapped(u_bar))
        for t in range(tiles):
            buf[t, depth] = energy

    def parameters(buf):
        left, right = [], []
        for v in range(views):
            u_bar = jnp.concatenate(gathered(buf, v * tiles, 0), axis=1)
            left.append(three_a(xbuf[v, 0:FEATS, :]))
            right.append(three_b(pick(u_bar, onehot[v], ((1,), (1,)))))
        out = dot16(
            jnp.concatenate(left, axis=0), jnp.concatenate(right, axis=0), ((0,), (0,))
        )
        return out[:params], lanes_total(buf, depth, everyone)[:, 0:1]

    image1 = image_tangent(gathered(f1_recv, 0, depth))
    cotangent(image1, b1_send)
    to_owners(b1_send, b1_recv, 2)

    if views > 1:
        landed(xbuf, views - 1, 0)
    for k in range(1, views):
        other = lax.rem(my_view + k, views)
        onehot[other] = place_matrix(
            [xbuf[other, FEATS + b : FEATS + 1 + b, :] for b in range(blocks)]
        )

    landed(b1_recv, everyone - 1, 2)
    product, energy = parameters(b1_recv)
    product = product + damped
    step1 = rr / (energy + rdr)
    residual = right - step1 * product
    put(f2_send, 0, swapped(pick(small_dot(proj, residual), mine)))
    sums = (
        jnp.where(lane == 0, total(residual * residual), 0.0)
        + jnp.where(lane == 1, total(damp * residual * residual), 0.0)
        + jnp.where(lane == 2, total(damped * residual), 0.0)
    )
    for t in range(tiles):
        f2_send[t, depth] = sums
    to_tiles(f2_send, f2_recv, 3)

    landed(f2_recv, tiles - 1, 3)
    sums = lanes_total(f2_recv, depth, tiles)
    rr1, sds, sdr = sums[:, 0:1], sums[:, 1:2], sums[:, 2:3]
    beta = rr1 / rr
    image2 = image_tangent(gathered(f2_recv, 0, 0)) + beta * image1
    cotangent(image2, b2_send)
    to_owners(b2_send, b2_recv, 4)

    direction = residual + beta * right
    landed(b2_recv, everyone - 1, 4)
    product, energy = parameters(b2_recv)
    product = product + damp * direction
    step2 = rr1 / (energy + sds + 2.0 * beta * sdr + beta * beta * rdr)
    sol_ref[...] = step1 * right + step2 * direction
    res_ref[...] = residual - step2 * product

    if views > 1:
        left(xbuf, views - 1, 0)
    left(f1_recv, tiles - 1, 1)
    left(b1_recv, everyone - 1, 2)
    left(f2_recv, tiles - 1, 3)
    left(b2_recv, everyone - 1, 4)


def solution(mesh):
    views, tiles = mesh.shape["views"], mesh.shape["tiles"]

    def body(*args):
        linear_point, right_side, damping, proj, basis, weight, order, dest, depths = args
        gauss, count = order.shape[2], dest.shape[1]
        capacity = max(2, count // tiles)
        width = gauss // count * capacity
        depth = FEATS * width // 128
        args = (
            linear_point,
            right_side,
            damping,
            jnp.swapaxes(proj[0], 0, 1),
            jnp.swapaxes(basis[0], 0, 1),
            weight[0],
            order[0],
            dest.reshape(1, count),
            depths,
        )
        shape = jax.ShapeDtypeStruct(linear_point.shape, F32)
        vmem = pl.BlockSpec(memory_space=pltpu.VMEM)
        first, later = 2 * depth + 1, depth + 1
        return pl.pallas_call(
            functools.partial(kernel, views, tiles),
            out_shape=(shape, shape),
            in_specs=[pl.BlockSpec(memory_space=pltpu.HBM)] * 9,
            out_specs=(vmem, vmem),
            scratch_shapes=[
                pltpu.VMEM((views, gauss, tiles * width), BF16),
                pltpu.VMEM((views, FEATS + 8, 128), F32),
                pltpu.VMEM((tiles, first, 1, 128), F32),
                pltpu.VMEM((tiles, first, 1, 128), F32),
                pltpu.VMEM((tiles, later, 1, 128), F32),
                pltpu.VMEM((views * tiles, later, 1, 128), F32),
                pltpu.VMEM((tiles, later, 1, 128), F32),
                pltpu.VMEM((tiles, later, 1, 128), F32),
                pltpu.VMEM((tiles, later, 1, 128), F32),
                pltpu.VMEM((views * tiles, later, 1, 128), F32),
            ]
            + [pltpu.VMEM(arg.shape, arg.dtype) for arg in args]
            + [
                pltpu.SemaphoreType.DMA((5,)),
                pltpu.SemaphoreType.DMA((5,)),
                pltpu.SemaphoreType.DMA((9,)),
            ],
            compiler_params=pltpu.CompilerParams(
                collective_id=0, has_side_effects=True, vmem_limit_bytes=63 * 1024 * 1024
            ),
        )(*args)

    in_specs = (
        P(None, "tiles"),
        P(None, "tiles"),
        P(None, "tiles"),
        P("views", None, None),
        P("views", "tiles", None, None),
        P("views", "tiles", None),
        P("views", "tiles", None),
        P("views", "tiles", None),
        P("views", "tiles"),
    )
    out_specs = (P(None, "tiles"), P(None, "tiles"))
    return jax.shard_map(body, mesh=mesh, in_specs=in_specs, out_specs=out_specs, check_vma=False)
```

```python
import functools

import jax
import jax.numpy as jnp
from jax import lax
from jax.experimental import pallas as pl
from jax.experimental.pallas import tpu as pltpu
from jax.sharding import PartitionSpec as P

MESH = pl.DeviceIdType.MESH
F32 = jnp.float32
BF16 = jnp.bfloat16
FEATS = 16
OFFSET = 6.0


def dot16(a, b, dims=((1,), (0,))):
    return lax.dot_general(a, b, (dims, ((), ())), preferred_element_type=F32)


def split(x):
    high = x.astype(BF16)
    return high, (x - high.astype(F32)).astype(BF16)


def stacked(x):
    return jnp.concatenate(split(x), axis=0)


def halves_sum(x):
    rows = x.shape[0] // 2
    return x[:rows] + x[rows:]


def pick(x, onehot, dims=((1,), (0,))):
    return halves_sum(dot16(stacked(x), onehot, dims))


def pick_left(twice, x):
    return dot16(twice, stacked(x))


def small_dot(a, b):
    high, low = split(b)
    left = stacked(a)
    return halves_sum(dot16(left, high)) + dot16(left[: a.shape[0]], low)


def wide_dot(a, pair):
    return halves_sum_wide(dot16(stacked(a), pair))


def halves_sum_wide(x):
    rows, lanes = x.shape[0] // 2, x.shape[1] // 2
    return x[:rows, :lanes] + x[rows:, :lanes] + x[:rows, lanes:]


def paired(x):
    return jnp.concatenate(split(x), axis=1)


def wide_dot_t(a, pair):
    high, low = split(a)
    left = jnp.concatenate(
        [
            jnp.concatenate([high, high], axis=1),
            jnp.concatenate([low, jnp.zeros_like(low)], axis=1),
        ],
        axis=0,
    )
    return halves_sum(dot16(left, pair, ((1,), (1,))))


def three_a(x):
    high, low = split(x)
    return jnp.concatenate([high, high, low], axis=0)


def three_b(x):
    high, low = split(x)
    return jnp.concatenate([high, low, high], axis=0)


def iota(shape, axis):
    return lax.broadcasted_iota(jnp.int32, shape, axis)


def total(x):
    return jnp.sum(jnp.sum(x, axis=0, keepdims=True), axis=1, keepdims=True)


def swap_blocks(x, width):
    groups = 128 // width
    depth = FEATS // groups
    rows, lanes = iota(x.shape, 0), iota(x.shape, 1)
    bit = 1
    while bit < groups:
        up, over = depth * bit, width * bit
        row_bit = (rows // up) % 2
        lane_bit = (lanes // over) % 2
        down = pltpu.roll(pltpu.roll(x, FEATS - up, 0), over, 1)
        back = pltpu.roll(pltpu.roll(x, up, 0), 128 - over, 1)
        x = jnp.where(row_bit == lane_bit, x, jnp.where(lane_bit == 1, down, back))
        bit *= 2
    return x


def kernel(
    views,
    tiles,
    *refs,
):
    my_view = lax.axis_index("views")
    me = lax.axis_index("tiles")
    flat = my_view * tiles + me
    everyone = views * tiles
    inputs, refs = refs[:9], refs[9:]
    res_ref, change_ref, coef1_ref, coef2_ref, onehot, xbuf = refs[:6]
    f1_send, f1_recv, b1_send, b1_recv, f2_send, f2_recv, b2_send, b2_recv = refs[6:14]
    held, (send_sem, recv_sem, in_sem) = refs[14:23], refs[23:]
    lp_ref, rs_ref, dm_ref, proj_ref, basis_ref, weight_ref, order_ref, dest_ref, depth_ref = held
    fetches = [
        pltpu.make_async_copy(inputs[i], held[i], in_sem.at[i]) for i in range(9)
    ]
    for i in (6, 7, 8, 3, 1, 0, 2, 4, 5):
        fetches[i].start()
    count = dest_ref.shape[1]
    gauss = order_ref.shape[1]
    params = rs_ref.shape[0]
    per = gauss // count
    capacity = max(2, count // tiles)
    width = per * capacity
    places = tiles * width
    blocks = places // 128
    groups = 128 // width
    depth = FEATS // groups

    def each(low, high, step):
        if high <= 32:
            for k in range(low, high):
                step(k, 0)
        else:
            lax.fori_loop(low, high, step, 0)

    barrier = pltpu.get_barrier_semaphore()

    def greet(k, carry):
        other = lax.rem(flat + k, everyone)
        pl.semaphore_signal(
            barrier, inc=1, device_id=(other // tiles, lax.rem(other, tiles)), device_id_type=MESH
        )
        return carry

    each(1, everyone, greet)

    eye = iota((count, count), 0) == iota((count, count), 1)
    for i in (6, 7, 8):
        fetches[i].wait()
    dest_row = dest_ref[...].astype(F32)
    dest = jnp.sum(jnp.where(eye, dest_row, 0.0), axis=1, keepdims=True)
    earlier = iota((count, count), 1) < iota((count, count), 0)
    position = jnp.sum(
        jnp.where((dest_row == dest) & earlier, 1.0, 0.0), axis=1, keepdims=True
    )
    slot = dest * float(capacity) + position
    mark = jnp.sum(jnp.where(eye, depth_ref[...].astype(F32), 0.0), axis=1, keepdims=True) + 1.0
    order = order_ref[...]
    own = iota((count, gauss), 1) // per == iota((count, gauss), 0)
    high = jnp.where(own, (order // 256).astype(F32), 0.0)
    low = jnp.where(own, (order % 256).astype(F32), 0.0)
    spread = (
        iota((gauss, 128), 0) % per == (iota((gauss, 128), 1) % width) // capacity
    ).astype(F32).astype(BF16)
    listed = dot16(jnp.concatenate([high, low], axis=0).astype(BF16), spread)
    listed = listed[:count] * 256.0 + listed[count:] + 1.0
    ids, marks = [], []
    for k in range(blocks):
        lane = iota((count, 128), 1) + k * 128
        wanted = (lane // width) * capacity + lane % capacity
        here = slot == wanted.astype(F32)
        ids.append(jnp.sum(jnp.where(here, listed, 0.0), axis=0, keepdims=True) - 1.0)
        marks.append(jnp.sum(jnp.where(here, mark, 0.0), axis=0, keepdims=True))

    def place_matrix(rows):
        numbers = iota((gauss, 128), 0).astype(F32)
        return jnp.concatenate(
            [(numbers == row).astype(F32).astype(BF16) for row in rows], axis=1
        )

    mine = place_matrix(ids)
    onehot[my_view] = mine
    for i in (3, 1, 0, 2, 4, 5):
        fetches[i].wait()
    proj = proj_ref[...]
    xbuf[my_view, 0:FEATS, 0:params] = proj
    for k in range(blocks):
        xbuf[my_view, FEATS + k : FEATS + 1 + k, :] = ids[k]

    right = rs_ref[...]
    damp = dm_ref[...]
    u_both = jnp.concatenate(
        [small_dot(proj, lp_ref[...]), small_dot(proj, right)], axis=0
    )
    u_both = pick(u_both, mine)
    damped = damp * right
    lane = iota((1, 128), 1)

    def put(buf, start, parts):
        for k in range(blocks):
            for row in range(FEATS):
                buf[k * groups + row // depth, start + row % depth] = parts[k][row : row + 1]

    def swapped(u):
        return [swap_blocks(u[:, k * 128 : k * 128 + 128], width) for k in range(blocks)]

    put(f1_send, 0, swapped(u_both[:FEATS]))
    put(f1_send, depth, swapped(u_both[FEATS:]))
    sums = jnp.where(lane == width, total(right * right), 0.0) + jnp.where(
        lane == width + 1, total(damped * right), 0.0
    )
    top = iota((FEATS, 128), 0) == 0
    for k in range(blocks):
        ranks = swap_blocks(jnp.where(top, marks[k], 0.0), width)
        for j in range(groups):
            f1_send[k * groups + j, 2 * depth] = ranks[j * depth : j * depth + 1] + sums

    pl.semaphore_wait(barrier, everyone - 1)

    def send(src, dst, view, tile, sem):
        return pltpu.make_async_remote_copy(
            src_ref=src,
            dst_ref=dst,
            send_sem=send_sem.at[sem],
            recv_sem=recv_sem.at[sem],
            device_id=(view, tile),
            device_id_type=MESH,
        )

    def to_tiles(src, dst, sem):
        def step(k, carry):
            other = lax.rem(me + k, tiles)
            send(src.at[other], dst.at[me], my_view, other, sem).start()
            return carry

        each(1, tiles, step)
        dst[me] = src[me]

    def to_owners(src, dst, sem):
        def step(k, carry):
            other = lax.rem(flat + k, everyone)
            tile = lax.rem(other, tiles)
            send(src.at[tile], dst.at[flat], other // tiles, tile, sem).start()
            return carry

        each(1, everyone, step)
        dst[flat] = src[me]

    def landed(dst, number, sem):
        whole = dst.at[pl.ds(0, number)]
        send(whole, whole, my_view, me, sem).wait_recv()

    def left(src, number, sem):
        whole = src.at[pl.ds(0, number)]
        send(whole, whole, my_view, me, sem).wait_send()

    to_tiles(f1_send, f1_recv, 1)
    for k in range(1, views):
        send(xbuf.at[my_view], xbuf.at[my_view], lax.rem(my_view + k, views), me, 0).start()

    basis = jnp.concatenate(
        [jnp.ones((1, 128), F32), jnp.zeros((3, 128), F32)]
        + [basis_ref[i] for i in range(FEATS - 4)],
        axis=0,
    )
    basis3 = three_b(basis)
    weight = weight_ref[...]
    color_row = (iota((FEATS, 128), 0) >= 1) & (iota((FEATS, 128), 0) <= 3)

    landed(f1_recv, tiles - 1, 1)

    def gathered(buf, first, start):
        out = []
        for k in range(blocks):
            rows = [
                buf[first + k * groups + row // depth, start + row % depth] for row in range(FEATS)
            ]
            out.append(swap_blocks(jnp.concatenate(rows, axis=0), width))
        return out

    def turned(parts):
        return jnp.concatenate([part.T for part in parts], axis=0)

    def turned3(parts):
        return turned([three_a(part).astype(F32) for part in parts]).astype(BF16)

    primal_parts = gathered(f1_recv, 0, 0)
    u0 = jnp.concatenate(primal_parts, axis=1)
    u0_t = turned3(primal_parts)
    ranks = []
    for k in range(blocks):
        rows = []
        for j in range(groups):
            row = f1_recv[k * groups + j, 2 * depth]
            rows.append(jnp.where(lane < width, row, 0.0))
            rows.append(jnp.zeros((depth - 1, 128), F32))
        ranks.append(swap_blocks(jnp.concatenate(rows, axis=0), width))
    marks_t = turned(ranks)[:, 0:1]

    def lanes_total(buf, row, number):
        out = buf[0, row]
        for t in range(1, number):
            out = out + buf[t, row]
        return out

    sums = lanes_total(f1_recv, 2 * depth, tiles)
    rr, rdr = sums[:, width : width + 1], sums[:, width + 1 : width + 2]

    halves = 8 // capacity
    steps = width // 8
    small = tiles * 8
    some = 4
    chunks = tiles // some
    rows = some * width
    sub = iota((some * steps, 8, 128), 1)

    def scan(x):
        x = x.reshape(some * steps, 8, 128)
        if halves == 2:
            moved = pltpu.roll(x, capacity, 1)
            before = jnp.where(sub >= capacity, moved, 0.0)
            through = x + moved
        else:
            through = inner = x
            step = 1
            while step < halves:
                shift = step * capacity
                inner = inner + jnp.where(sub >= shift, pltpu.roll(inner, shift, 1), 0.0)
                through = through + pltpu.roll(through, shift, 1)
                step *= 2
            before = inner - x
        through = through.reshape(some, steps, 8, 128)
        before = before.reshape(some, steps, 8, 128)
        run = through[:, 0]
        out = [before[:, 0]]
        for i in range(1, steps):
            out.append(before[:, i] + run)
            run = run + through[:, i]
        return jnp.stack(out, axis=1), run

    def wide(x):
        return x.reshape(some, 1, 8, 128)

    def full(x, c):
        return x[c * rows : c * rows + rows].reshape(some, steps, 8, x.shape[1])

    def slots(x, c):
        return x.reshape(tiles, 8, 128)[c * some : c * some + some]

    def joined(parts):
        return jnp.concatenate([x.reshape(some * 8, 128) for x in parts], axis=0)

    def pairs(x):
        return paired(x.reshape(rows, 128))

    mark_col = marks_t.reshape(tiles, width, 1)[:, 0:8, :].reshape(small, 1)
    square = (small, small)
    mark_row = jnp.sum(
        jnp.where(iota(square, 0) == iota(square, 1), mark_col, 0.0), axis=0, keepdims=True
    )
    first = (iota(square, 1) % 8) < capacity
    ahead = (first & (mark_row < mark_col) & (mark_row > 0.0)).astype(F32).astype(BF16)
    behind = (first & (mark_row > mark_col)).astype(F32).astype(BF16)
    ahead = jnp.concatenate([ahead, ahead], axis=1)
    behind = jnp.concatenate([behind, behind], axis=1)

    z_all = dot16(u0_t, basis3) - OFFSET
    alpha, before, through = [], [], []
    for c in range(chunks):
        z = full(z_all, c)
        filled = full(marks_t, c) > 0.0
        tail = jnp.exp(-jnp.abs(z))
        alpha.append(jnp.where(filled, jnp.where(z >= 0.0, 1.0, tail) / (1.0 + tail), 0.0))
        clear = jnp.where(filled, -(jnp.maximum(z, 0.0) + jnp.log(1.0 + tail)), 0.0)
        inner, whole = scan(clear)
        before.append(inner)
        through.append(whole)
    front = pick_left(ahead, joined(through))
    visible = [
        alpha[c] * jnp.exp(before[c] + wide(slots(front, c))) for c in range(chunks)
    ]
    visible_pair = jnp.concatenate([pairs(x) for x in visible], axis=0)

    def image_tangent(parts):
        du = jnp.concatenate(parts, axis=1)
        dz_all = dot16(turned3(parts), basis3)
        before, through, moved = [], [], []
        for c in range(chunks):
            inner, whole = scan(-alpha[c] * full(dz_all, c))
            before.append(inner)
            through.append(whole)
        front = pick_left(ahead, joined(through))
        for c in range(chunks):
            shift = before[c] + wide(slots(front, c))
            moved.append(
                pairs(visible[c] * ((1.0 - alpha[c]) * full(dz_all, c) + shift))
            )
        return wide_dot(du, visible_pair) + wide_dot(u0, jnp.concatenate(moved, axis=0))

    def cotangent(image, buf):
        image = jnp.where(color_row, image, 0.0)
        pull = image * weight
        energy = jnp.broadcast_to(total(pull * image), (1, 128))
        h_all = dot16(u0_t, three_b(pull))
        h, before, through, z_bar = [], [], [], []
        for c in range(chunks):
            h.append(full(h_all, c) * visible[c])
            inner, whole = scan(h[c])
            before.append(inner)
            through.append(whole)
        back = pick_left(behind, joined(through))
        for c in range(chunks):
            later = wide(through[c] + slots(back, c)) - before[c] - h[c]
            z_bar.append(pairs(h[c] * (1.0 - alpha[c]) - alpha[c] * later))
        u_bar = wide_dot_t(basis, jnp.concatenate(z_bar, axis=0)) + wide_dot_t(
            pull, visible_pair
        )
        put(buf, 0, swapped(u_bar))
        for t in range(tiles):
            buf[t, depth] = energy

    def parameters(buf):
        left, right = [], []
        for v in range(views):
            u_bar = jnp.concatenate(gathered(buf, v * tiles, 0), axis=1)
            left.append(three_a(xbuf[v, 0:FEATS, :]))
            right.append(three_b(pick(u_bar, onehot[v], ((1,), (1,)))))
        out = dot16(
            jnp.concatenate(left, axis=0), jnp.concatenate(right, axis=0), ((0,), (0,))
        )
        return out[:params], lanes_total(buf, depth, everyone)[:, 0:1]

    image1 = image_tangent(gathered(f1_recv, 0, depth))
    cotangent(image1, b1_send)
    to_owners(b1_send, b1_recv, 2)

    if views > 1:
        landed(xbuf, views - 1, 0)
    for k in range(1, views):
        other = lax.rem(my_view + k, views)
        onehot[other] = place_matrix(
            [xbuf[other, FEATS + b : FEATS + 1 + b, :] for b in range(blocks)]
        )

    landed(b1_recv, everyone - 1, 2)
    product, energy = parameters(b1_recv)
    product = product + damped
    step1 = rr / (energy + rdr)
    residual = right - step1 * product
    put(f2_send, 0, swapped(pick(small_dot(proj, residual), mine)))
    sums = (
        jnp.where(lane == 0, total(residual * residual), 0.0)
        + jnp.where(lane == 1, total(damp * residual * residual), 0.0)
        + jnp.where(lane == 2, total(damped * residual), 0.0)
    )
    for t in range(tiles):
        f2_send[t, depth] = sums
    to_tiles(f2_send, f2_recv, 3)

    landed(f2_recv, tiles - 1, 3)
    sums = lanes_total(f2_recv, depth, tiles)
    rr1, sds, sdr = sums[:, 0:1], sums[:, 1:2], sums[:, 2:3]
    beta = rr1 / rr
    image2 = image_tangent(gathered(f2_recv, 0, 0)) + beta * image1
    cotangent(image2, b2_send)
    to_owners(b2_send, b2_recv, 4)

    direction = residual + beta * right
    res_ref[...] = residual
    landed(b2_recv, everyone - 1, 4)
    product, energy = parameters(b2_recv)
    product = product + damp * direction
    step2 = rr1 / (energy + sds + 2.0 * beta * sdr + beta * beta * rdr)
    change_ref[...] = step2 * product
    coef1_ref[...] = jnp.broadcast_to(step1 + step2 * beta, (1, gauss))
    coef2_ref[...] = jnp.broadcast_to(step2, (1, gauss))

    if views > 1:
        left(xbuf, views - 1, 0)
    left(f1_recv, tiles - 1, 1)
    left(b1_recv, everyone - 1, 2)
    left(f2_recv, tiles - 1, 3)
    left(b2_recv, everyone - 1, 4)


def solution(mesh):
    views, tiles = mesh.shape["views"], mesh.shape["tiles"]

    def body(*args):
        linear_point, right_side, damping, proj, basis, weight, order, dest, depths = args
        gauss, count = order.shape[2], dest.shape[1]
        capacity = max(2, count // tiles)
        width = gauss // count * capacity
        depth = FEATS * width // 128
        args = (
            linear_point,
            right_side,
            damping,
            jnp.swapaxes(proj[0], 0, 1),
            jnp.swapaxes(basis[0], 0, 1),
            weight[0],
            order[0],
            dest.reshape(1, count),
            depths,
        )
        shape = jax.ShapeDtypeStruct(linear_point.shape, F32)
        vmem = pl.BlockSpec(memory_space=pltpu.VMEM)
        first, later = 2 * depth + 1, depth + 1
        coef = jax.ShapeDtypeStruct((1, gauss), F32)
        middle, change, coef1, coef2 = pl.pallas_call(
            functools.partial(kernel, views, tiles),
            out_shape=(shape, shape, coef, coef),
            in_specs=[pl.BlockSpec(memory_space=pltpu.HBM)] * 9,
            out_specs=(vmem,) * 4,
            scratch_shapes=[
                pltpu.VMEM((views, gauss, tiles * width), BF16),
                pltpu.VMEM((views, FEATS + 8, 128), F32),
                pltpu.VMEM((tiles, first, 1, 128), F32),
                pltpu.VMEM((tiles, first, 1, 128), F32),
                pltpu.VMEM((tiles, later, 1, 128), F32),
                pltpu.VMEM((views * tiles, later, 1, 128), F32),
                pltpu.VMEM((tiles, later, 1, 128), F32),
                pltpu.VMEM((tiles, later, 1, 128), F32),
                pltpu.VMEM((tiles, later, 1, 128), F32),
                pltpu.VMEM((views * tiles, later, 1, 128), F32),
            ]
            + [pltpu.VMEM(arg.shape, arg.dtype) for arg in args]
            + [
                pltpu.SemaphoreType.DMA((5,)),
                pltpu.SemaphoreType.DMA((5,)),
                pltpu.SemaphoreType.DMA((9,)),
            ],
            compiler_params=pltpu.CompilerParams(
                collective_id=0, has_side_effects=True, vmem_limit_bytes=63 * 1024 * 1024
            ),
        )(*args)
        return coef1 * right_side + coef2 * middle, middle - change

    in_specs = (
        P(None, "tiles"),
        P(None, "tiles"),
        P(None, "tiles"),
        P("views", None, None),
        P("views", "tiles", None, None),
        P("views", "tiles", None),
        P("views", "tiles", None),
        P("views", "tiles", None),
        P("views", "tiles"),
    )
    out_specs = (P(None, "tiles"), P(None, "tiles"))
    return jax.shard_map(body, mesh=mesh, in_specs=in_specs, out_specs=out_specs, check_vma=False)
```

```python
import functools

import jax
import jax.numpy as jnp
from jax import lax
from jax.experimental import pallas as pl
from jax.experimental.pallas import tpu as pltpu
from jax.sharding import PartitionSpec as P

MESH = pl.DeviceIdType.MESH
F32 = jnp.float32
BF16 = jnp.bfloat16
FEATS = 16
ITERS = 2
OFFSET = 6.0


def dot16(a, b, dims=((1,), (0,))):
    return lax.dot_general(a, b, (dims, ((), ())), preferred_element_type=F32)


def split(x):
    high = x.astype(BF16)
    return high, (x - high.astype(F32)).astype(BF16)


def stacked(x):
    return jnp.concatenate(split(x), axis=0)


def halves_sum(x):
    rows = x.shape[0] // 2
    return x[:rows] + x[rows:]


def pick(x, onehot, dims=((1,), (0,))):
    return halves_sum(dot16(stacked(x), onehot, dims))


def pick_left(twice, x):
    return dot16(twice, stacked(x))


def small_dot(a, b):
    high, low = split(b)
    left = stacked(a)
    return halves_sum(dot16(left, high)) + dot16(left[: a.shape[0]], low)


def wide_dot(a, pair):
    return halves_sum_wide(dot16(stacked(a), pair))


def halves_sum_wide(x):
    rows, lanes = x.shape[0] // 2, x.shape[1] // 2
    return x[:rows, :lanes] + x[rows:, :lanes] + x[:rows, lanes:]


def paired(x):
    return jnp.concatenate(split(x), axis=1)


def wide_dot_t(a, pair):
    high, low = split(a)
    left = jnp.concatenate(
        [
            jnp.concatenate([high, high], axis=1),
            jnp.concatenate([low, jnp.zeros_like(low)], axis=1),
        ],
        axis=0,
    )
    return halves_sum(dot16(left, pair, ((1,), (1,))))


def three_a(x):
    high, low = split(x)
    return jnp.concatenate([high, high, low], axis=0)


def three_b(x):
    high, low = split(x)
    return jnp.concatenate([high, low, high], axis=0)


def iota(shape, axis):
    return lax.broadcasted_iota(jnp.int32, shape, axis)


def total(x):
    return jnp.sum(jnp.sum(x, axis=0, keepdims=True), axis=1, keepdims=True)


def swap_blocks(x, width):
    groups = 128 // width
    depth = FEATS // groups
    rows, lanes = iota(x.shape, 0), iota(x.shape, 1)
    bit = 1
    while bit < groups:
        up, over = depth * bit, width * bit
        row_bit = (rows // up) % 2
        lane_bit = (lanes // over) % 2
        down = pltpu.roll(pltpu.roll(x, FEATS - up, 0), over, 1)
        back = pltpu.roll(pltpu.roll(x, up, 0), 128 - over, 1)
        x = jnp.where(row_bit == lane_bit, x, jnp.where(lane_bit == 1, down, back))
        bit *= 2
    return x


def kernel(
    views,
    tiles,
    *refs,
):
    my_view = lax.axis_index("views")
    me = lax.axis_index("tiles")
    flat = my_view * tiles + me
    everyone = views * tiles
    inputs, refs = refs[:9], refs[9:]
    sol_ref, res_ref, onehot, xbuf = refs[:4]
    p_send, p_recv, f_send, f_recv, b_send, b_recv = refs[4:10]
    tile_state, owner_state, held = refs[10:18], refs[18], refs[19:28]
    alpha_ref, visible_ref, pair_ref, u0_ref, u0t_ref, ahead_ref, behind_ref, image_ref = tile_state
    direction_ref = owner_state
    send_sem, recv_sem, in_sem = refs[28:]
    lp_ref, rs_ref, dm_ref, proj_ref, basis_ref, weight_ref, order_ref, dest_ref, depth_ref = held
    fetches = [
        pltpu.make_async_copy(inputs[i], held[i], in_sem.at[i]) for i in range(9)
    ]
    for i in (6, 7, 8, 3, 1, 0, 2, 4, 5):
        fetches[i].start()
    count = dest_ref.shape[1]
    gauss = order_ref.shape[1]
    params = rs_ref.shape[0]
    per = gauss // count
    capacity = max(2, count // tiles)
    width = per * capacity
    places = tiles * width
    blocks = places // 128
    groups = 128 // width
    depth = FEATS // groups

    barrier = pltpu.get_barrier_semaphore()

    def greet(k, carry):
        other = lax.rem(flat + k, everyone)
        pl.semaphore_signal(
            barrier, inc=1, device_id=(other // tiles, lax.rem(other, tiles)), device_id_type=MESH
        )
        return carry

    lax.fori_loop(1, everyone, greet, 0)

    eye = iota((count, count), 0) == iota((count, count), 1)
    for i in (6, 7, 8):
        fetches[i].wait()
    dest_row = dest_ref[...].astype(F32)
    dest = jnp.sum(jnp.where(eye, dest_row, 0.0), axis=1, keepdims=True)
    earlier = iota((count, count), 1) < iota((count, count), 0)
    position = jnp.sum(
        jnp.where((dest_row == dest) & earlier, 1.0, 0.0), axis=1, keepdims=True
    )
    slot = dest * float(capacity) + position
    mark = jnp.sum(jnp.where(eye, depth_ref[...].astype(F32), 0.0), axis=1, keepdims=True) + 1.0
    order = order_ref[...]
    own = iota((count, gauss), 1) // per == iota((count, gauss), 0)
    high = jnp.where(own, (order // 256).astype(F32), 0.0)
    low = jnp.where(own, (order % 256).astype(F32), 0.0)
    spread = (
        iota((gauss, 128), 0) % per == (iota((gauss, 128), 1) % width) // capacity
    ).astype(F32).astype(BF16)
    listed = dot16(jnp.concatenate([high, low], axis=0).astype(BF16), spread)
    listed = listed[:count] * 256.0 + listed[count:] + 1.0
    ids, marks = [], []
    for k in range(blocks):
        lane = iota((count, 128), 1) + k * 128
        wanted = (lane // width) * capacity + lane % capacity
        here = slot == wanted.astype(F32)
        ids.append(jnp.sum(jnp.where(here, listed, 0.0), axis=0, keepdims=True) - 1.0)
        marks.append(jnp.sum(jnp.where(here, mark, 0.0), axis=0, keepdims=True))

    def place_matrix(rows):
        numbers = iota((gauss, 128), 0).astype(F32)
        return jnp.concatenate(
            [(numbers == row).astype(F32).astype(BF16) for row in rows], axis=1
        )

    mine = place_matrix(ids)
    onehot[my_view] = mine
    for i in (3, 1, 0, 2, 4, 5):
        fetches[i].wait()
    proj = proj_ref[...]
    xbuf[my_view, 0:FEATS, 0:params] = proj
    for k in range(blocks):
        xbuf[my_view, FEATS + k : FEATS + 1 + k, :] = ids[k]

    u_primal = pick(small_dot(proj, lp_ref[...]), mine)
    lane = iota((1, 128), 1)

    def put(buf, parts, extra):
        for k in range(blocks):
            for j in range(groups):
                t = k * groups + j
                buf[t, 0:depth, :] = parts[k][j * depth : j * depth + depth]
                buf[t, depth : depth + 1, :] = extra[t]

    def swapped(u):
        return [swap_blocks(u[:, k * 128 : k * 128 + 128], width) for k in range(blocks)]

    top = iota((FEATS, 128), 0) == 0
    extra = []
    for k in range(blocks):
        ranks = swap_blocks(jnp.where(top, marks[k], 0.0), width)
        extra += [ranks[j * depth : j * depth + 1] for j in range(groups)]
    put(p_send, swapped(u_primal), extra)
    res_ref[...] = rs_ref[...]
    sol_ref[...] = jnp.zeros_like(sol_ref)
    direction_ref[...] = jnp.zeros_like(direction_ref)
    image_ref[...] = jnp.zeros_like(image_ref)

    pl.semaphore_wait(barrier, everyone - 1)

    def send(src, dst, view, tile, sem):
        return pltpu.make_async_remote_copy(
            src_ref=src,
            dst_ref=dst,
            send_sem=send_sem.at[sem],
            recv_sem=recv_sem.at[sem],
            device_id=(view, tile),
            device_id_type=MESH,
        )

    def part(buf, number):
        return buf.at[number, pl.ds(0, depth + 1)]

    def to_tiles(src, dst, sem):
        def step(k, carry):
            other = lax.rem(me + k, tiles)
            send(part(src, other), part(dst, me), my_view, other, sem).start()
            return carry

        lax.fori_loop(1, tiles, step, 0)
        dst[me] = src[me]

    def to_owners(src, dst, sem):
        def step(k, carry):
            other = lax.rem(flat + k, everyone)
            tile = lax.rem(other, tiles)
            send(part(src, tile), part(dst, flat), other // tiles, tile, sem).start()
            return carry

        lax.fori_loop(1, everyone, step, 0)
        dst[flat] = src[me]

    def landed(dst, number, sem):
        whole = dst.at[pl.ds(0, number), pl.ds(0, depth + 1)]
        send(whole, whole, my_view, me, sem).wait_recv()

    def left(src, number, sem):
        whole = src.at[pl.ds(0, number), pl.ds(0, depth + 1)]
        send(whole, whole, my_view, me, sem).wait_send()

    to_tiles(p_send, p_recv, 1)
    for k in range(1, views):
        send(xbuf.at[my_view], xbuf.at[my_view], lax.rem(my_view + k, views), me, 0).start()

    basis = jnp.concatenate(
        [jnp.ones((1, 128), F32), jnp.zeros((3, 128), F32)]
        + [basis_ref[i] for i in range(FEATS - 4)],
        axis=0,
    )
    basis3 = three_b(basis)
    weight = weight_ref[...]
    color_row = (iota((FEATS, 128), 0) >= 1) & (iota((FEATS, 128), 0) <= 3)

    def gathered(buf, first):
        out = []
        for k in range(blocks):
            lines = [buf[first + k * groups + j, 0:depth, :] for j in range(groups)]
            out.append(swap_blocks(jnp.concatenate(lines, axis=0), width))
        return out

    def turned(parts):
        return jnp.concatenate([part.T for part in parts], axis=0)

    def turned3(parts):
        return turned([three_a(part).astype(F32) for part in parts]).astype(BF16)

    def lanes_total(buf, row, number):
        return jnp.sum(buf[0:number], axis=0)[row : row + 1]

    halves = 8 // capacity
    steps = width // 8
    small = tiles * 8
    some = 4
    chunks = tiles // some
    rows = some * width
    sub = iota((some * steps, 8, 128), 1)

    def scan(x):
        x = x.reshape(some * steps, 8, 128)
        if halves == 2:
            moved = pltpu.roll(x, capacity, 1)
            before = jnp.where(sub >= capacity, moved, 0.0)
            through = x + moved
        else:
            through = inner = x
            step = 1
            while step < halves:
                shift = step * capacity
                inner = inner + jnp.where(sub >= shift, pltpu.roll(inner, shift, 1), 0.0)
                through = through + pltpu.roll(through, shift, 1)
                step *= 2
            before = inner - x
        through = through.reshape(some, steps, 8, 128)
        before = before.reshape(some, steps, 8, 128)
        run = through[:, 0]
        out = [before[:, 0]]
        for i in range(1, steps):
            out.append(before[:, i] + run)
            run = run + through[:, i]
        return jnp.stack(out, axis=1), run

    def wide(x):
        return x.reshape(some, 1, 8, 128)

    def full(x, c):
        return x[c * rows : c * rows + rows].reshape(some, steps, 8, x.shape[1])

    def slots(x, c):
        return x.reshape(tiles, 8, 128)[c * some : c * some + some]

    def joined(parts):
        return jnp.concatenate([x.reshape(some * 8, 128) for x in parts], axis=0)

    def pairs(x):
        return paired(x.reshape(rows, 128))

    def primal():
        landed(p_recv, tiles - 1, 1)
        primal_parts = gathered(p_recv, 0)
        u0 = jnp.concatenate(primal_parts, axis=1)
        u0_ref[...] = u0
        u0_t = turned3(primal_parts)
        u0t_ref[...] = u0_t
        ranks = []
        for k in range(blocks):
            lines = []
            for j in range(groups):
                lines.append(p_recv[k * groups + j, depth : depth + 1, :])
                lines.append(jnp.zeros((depth - 1, 128), F32))
            ranks.append(swap_blocks(jnp.concatenate(lines, axis=0), width))
        marks_t = turned(ranks)[:, 0:1]
        mark_col = marks_t.reshape(tiles, width, 1)[:, 0:8, :].reshape(small, 1)
        square = (small, small)
        mark_row = jnp.sum(
            jnp.where(iota(square, 0) == iota(square, 1), mark_col, 0.0), axis=0, keepdims=True
        )
        first = (iota(square, 1) % 8) < capacity
        ahead = (first & (mark_row < mark_col) & (mark_row > 0.0)).astype(F32).astype(BF16)
        behind = (first & (mark_row > mark_col)).astype(F32).astype(BF16)
        ahead = jnp.concatenate([ahead, ahead], axis=1)
        ahead_ref[...] = ahead
        behind_ref[...] = jnp.concatenate([behind, behind], axis=1)

        z_all = dot16(u0_t, basis3) - OFFSET
        alpha, before, through = [], [], []
        for c in range(chunks):
            z = full(z_all, c)
            filled = full(marks_t, c) > 0.0
            tail = jnp.exp(-jnp.abs(z))
            alpha.append(jnp.where(filled, jnp.where(z >= 0.0, 1.0, tail) / (1.0 + tail), 0.0))
            clear = jnp.where(filled, -(jnp.maximum(z, 0.0) + jnp.log(1.0 + tail)), 0.0)
            inner, whole = scan(clear)
            before.append(inner)
            through.append(whole)
        front = pick_left(ahead, joined(through))
        for c in range(chunks):
            seen = alpha[c] * jnp.exp(before[c] + wide(slots(front, c)))
            alpha_ref[c] = alpha[c]
            visible_ref[c] = seen
            pair_ref[c * rows : c * rows + rows, :] = pairs(seen)

    def image_tangent(parts):
        du = jnp.concatenate(parts, axis=1)
        dz_all = dot16(turned3(parts), basis3)
        before, through, moved = [], [], []
        for c in range(chunks):
            inner, whole = scan(-alpha_ref[c] * full(dz_all, c))
            before.append(inner)
            through.append(whole)
        front = pick_left(ahead_ref[...], joined(through))
        for c in range(chunks):
            shift = before[c] + wide(slots(front, c))
            moved.append(
                pairs(visible_ref[c] * ((1.0 - alpha_ref[c]) * full(dz_all, c) + shift))
            )
        return wide_dot(du, pair_ref[...]) + wide_dot(u0_ref[...], jnp.concatenate(moved, axis=0))

    def cotangent(image, buf):
        image = jnp.where(color_row, image, 0.0)
        pull = image * weight
        energy = jnp.broadcast_to(total(pull * image), (1, 128))
        h_all = dot16(u0t_ref[...], three_b(pull))
        h, before, through, z_bar = [], [], [], []
        for c in range(chunks):
            h.append(full(h_all, c) * visible_ref[c])
            inner, whole = scan(h[c])
            before.append(inner)
            through.append(whole)
        back = pick_left(behind_ref[...], joined(through))
        for c in range(chunks):
            later = wide(through[c] + slots(back, c)) - before[c] - h[c]
            z_bar.append(pairs(h[c] * (1.0 - alpha_ref[c]) - alpha_ref[c] * later))
        u_bar = wide_dot_t(basis, jnp.concatenate(z_bar, axis=0)) + wide_dot_t(
            pull, pair_ref[...]
        )
        put(buf, swapped(u_bar), [energy] * tiles)

    def parameters(buf):
        left, right = [], []
        for v in range(views):
            u_bar = jnp.concatenate(gathered(buf, v * tiles), axis=1)
            left.append(three_a(xbuf[v, 0:FEATS, :]))
            right.append(three_b(pick(u_bar, onehot[v], ((1,), (1,)))))
        out = dot16(
            jnp.concatenate(left, axis=0), jnp.concatenate(right, axis=0), ((0,), (0,))
        )
        return out[:params], lanes_total(buf, depth, everyone)[:, 0:1]

    def other_views():
        whole = xbuf.at[pl.ds(0, views - 1)]
        send(whole, whole, my_view, me, 0).wait_recv()
        for k in range(1, views):
            other = lax.rem(my_view + k, views)
            onehot[other] = place_matrix(
                [xbuf[other, FEATS + b : FEATS + 1 + b, :] for b in range(blocks)]
            )

    def iterate(turn, carry):
        rr_old, old_damped = carry
        residual = res_ref[...]
        u = swapped(pick(small_dot(proj, residual), onehot[my_view]))
        damped_residual = dm_ref[...] * residual
        sums = (
            jnp.where(lane == 0, total(residual * residual), 0.0)
            + jnp.where(lane == 1, total(damped_residual * residual), 0.0)
            + jnp.where(lane == 2, total(damped_residual * direction_ref[...]), 0.0)
        )
        put(f_send.at[turn], u, [sums] * tiles)
        to_tiles(f_send.at[turn], f_recv.at[turn], 2 + turn)

        @pl.when(turn == 0)
        def _():
            primal()

        landed(f_recv.at[turn], tiles - 1, 2 + turn)
        sums = lanes_total(f_recv.at[turn], depth, tiles)
        rr = sums[:, 0:1]
        beta = jnp.where(turn == 0, 0.0, rr / rr_old)
        image = image_tangent(gathered(f_recv.at[turn], 0)) + beta * image_ref[...]
        image_ref[...] = image
        cotangent(image, b_send.at[turn])
        to_owners(b_send.at[turn], b_recv.at[turn], 2 + ITERS + turn)
        direction = residual + beta * direction_ref[...]
        direction_ref[...] = direction
        both_damped = sums[:, 1:2] + 2.0 * beta * sums[:, 2:3] + beta * beta * old_damped
        if views > 1:
            pl.when(turn == 0)(other_views)

        landed(b_recv.at[turn], everyone - 1, 2 + ITERS + turn)
        product, energy = parameters(b_recv.at[turn])
        product = product + dm_ref[...] * direction
        step = rr / (energy + both_damped)
        sol_ref[...] += step * direction
        res_ref[...] = residual - step * product
        return rr, both_damped

    lax.fori_loop(0, ITERS, iterate, (jnp.ones((1, 1), F32), jnp.zeros((1, 1), F32)))

    if views > 1:
        whole = xbuf.at[pl.ds(0, views - 1)]
        send(whole, whole, my_view, me, 0).wait_send()
    left(p_recv, tiles - 1, 1)
    for turn in range(ITERS):
        left(f_recv.at[turn], tiles - 1, 2 + turn)
        left(b_recv.at[turn], everyone - 1, 2 + ITERS + turn)


def store(a_ref, b_ref, a_out, b_out, a_held, b_held, sem):
    rows = a_ref.shape[0]
    half = rows // 16 * 8
    parts = []
    for src, mid, out in ((a_ref, a_held, a_out), (b_ref, b_held, b_out)):
        for place in (pl.ds(0, half), pl.ds(half, rows - half)):
            number = len(parts)
            parts.append(
                (
                    pltpu.make_async_copy(src.at[place], mid.at[place], sem.at[0, number]),
                    pltpu.make_async_copy(mid.at[place], out.at[place], sem.at[1, number]),
                )
            )
    for come, go in parts:
        come.start()
    for come, go in parts:
        come.wait()
        go.start()
    for come, go in parts:
        go.wait()


def solution(mesh):
    views, tiles = mesh.shape["views"], mesh.shape["tiles"]

    def body(*args):
        linear_point, right_side, damping, proj, basis, weight, order, dest, depths = args
        gauss, count = order.shape[2], dest.shape[1]
        capacity = max(2, count // tiles)
        width = gauss // count * capacity
        depth = FEATS * width // 128
        args = (
            linear_point,
            right_side,
            damping,
            jnp.swapaxes(proj[0], 0, 1),
            jnp.swapaxes(basis[0], 0, 1),
            weight[0],
            order[0],
            dest.reshape(1, count),
            depths,
        )
        shape = jax.ShapeDtypeStruct(linear_point.shape, F32)
        vmem = pl.BlockSpec(memory_space=pltpu.VMEM)
        places = tiles * width
        message = (8, 128)
        chunk = (tiles // 4, 4, width // 8, 8, 128)
        results = pl.pallas_call(
            functools.partial(kernel, views, tiles),
            out_shape=(shape, shape),
            in_specs=[pl.BlockSpec(memory_space=pltpu.HBM)] * 9,
            out_specs=(vmem, vmem),
            scratch_shapes=[
                pltpu.VMEM((views, gauss, places), BF16),
                pltpu.VMEM((views, FEATS + 8, 128), F32),
                pltpu.VMEM((tiles,) + message, F32),
                pltpu.VMEM((tiles,) + message, F32),
                pltpu.VMEM((ITERS, tiles) + message, F32),
                pltpu.VMEM((ITERS, tiles) + message, F32),
                pltpu.VMEM((ITERS, tiles) + message, F32),
                pltpu.VMEM((ITERS, views * tiles) + message, F32),
                pltpu.VMEM(chunk, F32),
                pltpu.VMEM(chunk, F32),
                pltpu.VMEM((places, 256), BF16),
                pltpu.VMEM((FEATS, places), F32),
                pltpu.VMEM((places, 3 * FEATS), BF16),
                pltpu.VMEM((tiles * 8, tiles * 16), BF16),
                pltpu.VMEM((tiles * 8, tiles * 16), BF16),
                pltpu.VMEM((FEATS, 128), F32),
                pltpu.VMEM(linear_point.shape, F32),
            ]
            + [pltpu.VMEM(arg.shape, arg.dtype) for arg in args]
            + [
                pltpu.SemaphoreType.DMA((2 + 2 * ITERS,)),
                pltpu.SemaphoreType.DMA((2 + 2 * ITERS,)),
                pltpu.SemaphoreType.DMA((9,)),
            ],
            compiler_params=pltpu.CompilerParams(
                collective_id=0, has_side_effects=True, vmem_limit_bytes=63 * 1024 * 1024
            ),
        )(*args)
        return pl.pallas_call(
            store,
            out_shape=(shape, shape),
            in_specs=[pl.BlockSpec(memory_space=pltpu.HBM)] * 2,
            out_specs=(pl.BlockSpec(memory_space=pltpu.HBM),) * 2,
            scratch_shapes=[
                pltpu.VMEM(shape.shape, F32),
                pltpu.VMEM(shape.shape, F32),
                pltpu.SemaphoreType.DMA((2, 4)),
            ],
            compiler_params=pltpu.CompilerParams(vmem_limit_bytes=63 * 1024 * 1024),
        )(*results)

    in_specs = (
        P(None, "tiles"),
        P(None, "tiles"),
        P(None, "tiles"),
        P("views", None, None),
        P("views", "tiles", None, None),
        P("views", "tiles", None),
        P("views", "tiles", None),
        P("views", "tiles", None),
        P("views", "tiles"),
    )
    out_specs = (P(None, "tiles"), P(None, "tiles"))
    return jax.shard_map(body, mesh=mesh, in_specs=in_specs, out_specs=out_specs, check_vma=False)
```

```python
import functools

import jax
import jax.numpy as jnp
from jax import lax
from jax.experimental import pallas as pl
from jax.experimental.pallas import tpu as pltpu
from jax.sharding import PartitionSpec as P

MESH = pl.DeviceIdType.MESH
F32 = jnp.float32
BF16 = jnp.bfloat16
FEATS = 16
OFFSET = 6.0


def dot16(a, b, dims=((1,), (0,))):
    return lax.dot_general(a, b, (dims, ((), ())), preferred_element_type=F32)


def split(x):
    high = x.astype(BF16)
    return high, (x - high.astype(F32)).astype(BF16)


def stacked(x):
    return jnp.concatenate(split(x), axis=0)


def halves_sum(x):
    rows = x.shape[0] // 2
    return x[:rows] + x[rows:]


def pick(x, onehot, dims=((1,), (0,))):
    return halves_sum(dot16(stacked(x), onehot, dims))


def pick_left(twice, x):
    return dot16(twice, stacked(x))


def small_dot(a, b):
    high, low = split(b)
    left = stacked(a)
    return halves_sum(dot16(left, high)) + dot16(left[: a.shape[0]], low)


def wide_dot(a, pair):
    return halves_sum_wide(dot16(stacked(a), pair))


def halves_sum_wide(x):
    rows, lanes = x.shape[0] // 2, x.shape[1] // 2
    return x[:rows, :lanes] + x[rows:, :lanes] + x[:rows, lanes:]


def paired(x):
    return jnp.concatenate(split(x), axis=1)


def wide_dot_t(a, pair):
    high, low = split(a)
    left = jnp.concatenate(
        [
            jnp.concatenate([high, high], axis=1),
            jnp.concatenate([low, jnp.zeros_like(low)], axis=1),
        ],
        axis=0,
    )
    return halves_sum(dot16(left, pair, ((1,), (1,))))


def three_a(x):
    high, low = split(x)
    return jnp.concatenate([high, high, low], axis=0)


def three_b(x):
    high, low = split(x)
    return jnp.concatenate([high, low, high], axis=0)


def iota(shape, axis):
    return lax.broadcasted_iota(jnp.int32, shape, axis)


def total(x):
    return jnp.sum(jnp.sum(x, axis=0, keepdims=True), axis=1, keepdims=True)


def swap_blocks(x, width):
    groups = 128 // width
    depth = FEATS // groups
    rows, lanes = iota(x.shape, 0), iota(x.shape, 1)
    bit = 1
    while bit < groups:
        up, over = depth * bit, width * bit
        row_bit = (rows // up) % 2
        lane_bit = (lanes // over) % 2
        down = pltpu.roll(pltpu.roll(x, FEATS - up, 0), over, 1)
        back = pltpu.roll(pltpu.roll(x, up, 0), 128 - over, 1)
        x = jnp.where(row_bit == lane_bit, x, jnp.where(lane_bit == 1, down, back))
        bit *= 2
    return x


def kernel(
    views,
    tiles,
    *refs,
):
    my_view = lax.axis_index("views")
    me = lax.axis_index("tiles")
    flat = my_view * tiles + me
    everyone = views * tiles
    inputs, refs = refs[:9], refs[9:]
    sol_ref, res_ref, onehot, xbuf = refs[:4]
    f1_send, f1_recv, b1_send, b1_recv, f2_send, f2_recv, b2_send, b2_recv = refs[4:12]
    held, (send_sem, recv_sem, in_sem) = refs[12:21], refs[21:]
    lp_ref, rs_ref, dm_ref, proj_ref, basis_ref, weight_ref, order_ref, dest_ref, depth_ref = held
    fetches = [
        pltpu.make_async_copy(inputs[i], held[i], in_sem.at[i]) for i in range(9)
    ]
    for i in (6, 7, 8, 3, 1, 0, 2, 4, 5):
        fetches[i].start()
    count = dest_ref.shape[1]
    gauss = order_ref.shape[1]
    params = rs_ref.shape[0]
    per = gauss // count
    capacity = max(2, count // tiles)
    width = per * capacity
    places = tiles * width
    blocks = places // 128
    groups = 128 // width
    depth = FEATS // groups

    barrier = pltpu.get_barrier_semaphore()

    def greet(k, carry):
        other = lax.rem(flat + k, everyone)
        pl.semaphore_signal(
            barrier, inc=1, device_id=(other // tiles, lax.rem(other, tiles)), device_id_type=MESH
        )
        return carry

    lax.fori_loop(1, everyone, greet, 0)

    eye = iota((count, count), 0) == iota((count, count), 1)
    for i in (6, 7, 8):
        fetches[i].wait()
    dest_row = dest_ref[...].astype(F32)
    dest = jnp.sum(jnp.where(eye, dest_row, 0.0), axis=1, keepdims=True)
    earlier = iota((count, count), 1) < iota((count, count), 0)
    position = jnp.sum(
        jnp.where((dest_row == dest) & earlier, 1.0, 0.0), axis=1, keepdims=True
    )
    slot = dest * float(capacity) + position
    mark = jnp.sum(jnp.where(eye, depth_ref[...].astype(F32), 0.0), axis=1, keepdims=True) + 1.0
    order = order_ref[...]
    own = iota((count, gauss), 1) // per == iota((count, gauss), 0)
    high = jnp.where(own, (order // 256).astype(F32), 0.0)
    low = jnp.where(own, (order % 256).astype(F32), 0.0)
    spread = (
        iota((gauss, 128), 0) % per == (iota((gauss, 128), 1) % width) // capacity
    ).astype(F32).astype(BF16)
    listed = dot16(jnp.concatenate([high, low], axis=0).astype(BF16), spread)
    listed = listed[:count] * 256.0 + listed[count:] + 1.0
    ids, marks = [], []
    for k in range(blocks):
        lane = iota((count, 128), 1) + k * 128
        wanted = (lane // width) * capacity + lane % capacity
        here = slot == wanted.astype(F32)
        ids.append(jnp.sum(jnp.where(here, listed, 0.0), axis=0, keepdims=True) - 1.0)
        marks.append(jnp.sum(jnp.where(here, mark, 0.0), axis=0, keepdims=True))

    def place_matrix(rows):
        numbers = iota((gauss, 128), 0).astype(F32)
        return jnp.concatenate(
            [(numbers == row).astype(F32).astype(BF16) for row in rows], axis=1
        )

    mine = place_matrix(ids)
    onehot[my_view] = mine
    for i in (3, 1, 0, 2, 4, 5):
        fetches[i].wait()
    proj = proj_ref[...]
    xbuf[my_view, 0:FEATS, 0:params] = proj
    for k in range(blocks):
        xbuf[my_view, FEATS + k : FEATS + 1 + k, :] = ids[k]

    right = rs_ref[...]
    damp = dm_ref[...]
    u_both = jnp.concatenate(
        [small_dot(proj, lp_ref[...]), small_dot(proj, right)], axis=0
    )
    u_both = pick(u_both, mine)
    damped = damp * right
    lane = iota((1, 128), 1)

    def put(buf, start, parts):
        for k in range(blocks):
            for row in range(FEATS):
                buf[k * groups + row // depth, start + row % depth] = parts[k][row : row + 1]

    def swapped(u):
        return [swap_blocks(u[:, k * 128 : k * 128 + 128], width) for k in range(blocks)]

    put(f1_send, 0, swapped(u_both[:FEATS]))
    put(f1_send, depth, swapped(u_both[FEATS:]))
    sums = jnp.where(lane == width, total(right * right), 0.0) + jnp.where(
        lane == width + 1, total(damped * right), 0.0
    )
    top = iota((FEATS, 128), 0) == 0
    for k in range(blocks):
        ranks = swap_blocks(jnp.where(top, marks[k], 0.0), width)
        for j in range(groups):
            f1_send[k * groups + j, 2 * depth] = ranks[j * depth : j * depth + 1] + sums

    pl.semaphore_wait(barrier, everyone - 1)

    def send(src, dst, view, tile, sem):
        return pltpu.make_async_remote_copy(
            src_ref=src,
            dst_ref=dst,
            send_sem=send_sem.at[sem],
            recv_sem=recv_sem.at[sem],
            device_id=(view, tile),
            device_id_type=MESH,
        )

    half = tiles // 2
    far, near = (1 - me // half) * half, (me // half) * half

    def to_tiles(src, dst, sem):
        def start(other):
            send(src.at[other], dst.at[me], my_view, other, sem).start()

        def across(k, carry):
            start(far + lax.rem(me + k, half))
            return carry

        def along(k, carry):
            start(near + lax.rem(me + k, half))
            return carry

        lax.fori_loop(0, half, across, 0)
        lax.fori_loop(1, half, along, 0)
        dst[me] = src[me]

    def to_owners(src, dst, sem):
        def start(view, tile):
            send(src.at[tile], dst.at[flat], view, tile, sem).start()

        def across(k, carry):
            view = lax.rem(my_view + 1 + k // half, views)
            start(view, far + lax.rem(me + k, half))
            return carry

        def beside(k, carry):
            view = lax.rem(my_view + 1 + k // half, views)
            start(view, near + lax.rem(me + k, half))
            return carry

        def along(k, carry):
            start(my_view, near + lax.rem(me + k, half))
            return carry

        lax.fori_loop(0, views * half, across, 0)
        lax.fori_loop(0, (views - 1) * half, beside, 0)
        lax.fori_loop(1, half, along, 0)
        dst[flat] = src[me]

    def landed(dst, number, sem):
        whole = dst.at[pl.ds(0, number)]
        send(whole, whole, my_view, me, sem).wait_recv()

    def left(src, number, sem):
        whole = src.at[pl.ds(0, number)]
        send(whole, whole, my_view, me, sem).wait_send()

    to_tiles(f1_send, f1_recv, 1)
    for k in range(1, views):
        send(xbuf.at[my_view], xbuf.at[my_view], lax.rem(my_view + k, views), me, 0).start()

    basis = jnp.concatenate(
        [jnp.ones((1, 128), F32), jnp.zeros((3, 128), F32)]
        + [basis_ref[i] for i in range(FEATS - 4)],
        axis=0,
    )
    basis3 = three_b(basis)
    weight = weight_ref[...]
    color_row = (iota((FEATS, 128), 0) >= 1) & (iota((FEATS, 128), 0) <= 3)

    landed(f1_recv, tiles - 1, 1)

    def gathered(buf, first, start):
        out = []
        for k in range(blocks):
            rows = [
                buf[first + k * groups + row // depth, start + row % depth] for row in range(FEATS)
            ]
            out.append(swap_blocks(jnp.concatenate(rows, axis=0), width))
        return out

    def turned(parts):
        return jnp.concatenate([part.T for part in parts], axis=0)

    def turned3(parts):
        return turned([three_a(part).astype(F32) for part in parts]).astype(BF16)

    primal_parts = gathered(f1_recv, 0, 0)
    u0 = jnp.concatenate(primal_parts, axis=1)
    u0_t = turned3(primal_parts)
    ranks = []
    for k in range(blocks):
        rows = []
        for j in range(groups):
            row = f1_recv[k * groups + j, 2 * depth]
            rows.append(jnp.where(lane < width, row, 0.0))
            rows.append(jnp.zeros((depth - 1, 128), F32))
        ranks.append(swap_blocks(jnp.concatenate(rows, axis=0), width))
    marks_t = turned(ranks)[:, 0:1]

    def lanes_total(buf, row, number):
        out = buf[0, row]
        for t in range(1, number):
            out = out + buf[t, row]
        return out

    sums = lanes_total(f1_recv, 2 * depth, tiles)
    rr, rdr = sums[:, width : width + 1], sums[:, width + 1 : width + 2]

    halves = 8 // capacity
    steps = width // 8
    small = tiles * 8
    sub = iota((tiles * steps, 8, 128), 1)

    def scan(x):
        x = x.reshape(tiles * steps, 8, 128)
        through = inner = x
        step = 1
        while step < halves:
            shift = step * capacity
            inner = inner + jnp.where(sub >= shift, pltpu.roll(inner, shift, 1), 0.0)
            through = through + pltpu.roll(through, shift, 1)
            step *= 2
        before = inner - x
        through = through.reshape(tiles, steps, 8, 128)
        before = before.reshape(tiles, steps, 8, 128)
        run = jnp.zeros((tiles, 8, 128), F32)
        out = []
        for i in range(steps):
            out.append(before[:, i] + run)
            run = run + through[:, i]
        return jnp.stack(out, axis=1), run

    def wide(x):
        return x.reshape(tiles, 1, 8, 128)

    def full(x):
        return x.reshape(tiles, steps, 8, 128)

    mark_col = marks_t.reshape(tiles, width, 1)[:, 0:8, :].reshape(small, 1)
    square = (small, small)
    mark_row = jnp.sum(
        jnp.where(iota(square, 0) == iota(square, 1), mark_col, 0.0), axis=0, keepdims=True
    )
    first = (iota(square, 1) % 8) < capacity
    ahead = (first & (mark_row < mark_col) & (mark_row > 0.0)).astype(F32).astype(BF16)
    behind = (first & (mark_row > mark_col)).astype(F32).astype(BF16)
    ahead = jnp.concatenate([ahead, ahead], axis=1)
    behind = jnp.concatenate([behind, behind], axis=1)

    z = dot16(u0_t, basis3) - OFFSET
    filled = marks_t > 0.0
    tail = jnp.exp(-jnp.abs(z))
    alpha = jnp.where(filled, jnp.where(z >= 0.0, 1.0, tail) / (1.0 + tail), 0.0)
    clear = jnp.where(filled, -(jnp.maximum(z, 0.0) + jnp.log(1.0 + tail)), 0.0)
    before, through = scan(clear)
    before = before + wide(pick_left(ahead, through.reshape(small, 128)))
    visible = full(alpha) * jnp.exp(before)
    visible_pair = paired(visible.reshape(places, 128))
    alpha = full(alpha)
    rest = 1.0 - alpha

    def image_tangent(parts):
        du = jnp.concatenate(parts, axis=1)
        dz = full(dot16(turned3(parts), basis3))
        before, through = scan(-alpha * dz)
        before = before + wide(pick_left(ahead, through.reshape(small, 128)))
        moved = visible * (rest * dz + before)
        return wide_dot(du, visible_pair) + wide_dot(u0, paired(moved.reshape(places, 128)))

    def cotangent(image, buf):
        image = jnp.where(color_row, image, 0.0)
        pull = image * weight
        energy = jnp.broadcast_to(total(pull * image), (1, 128))
        h = full(dot16(u0_t, three_b(pull))) * visible
        before, through = scan(h)
        later = through + pick_left(behind, through.reshape(small, 128)).reshape(tiles, 8, 128)
        z_bar = h * rest - alpha * (wide(later) - before - h)
        u_bar = wide_dot_t(basis, paired(z_bar.reshape(places, 128))) + wide_dot_t(
            pull, visible_pair
        )
        put(buf, 0, swapped(u_bar))
        for t in range(tiles):
            buf[t, depth] = energy

    def parameters(buf):
        left, right = [], []
        for v in range(views):
            u_bar = jnp.concatenate(gathered(buf, v * tiles, 0), axis=1)
            left.append(three_a(xbuf[v, 0:FEATS, :]))
            right.append(three_b(pick(u_bar, onehot[v], ((1,), (1,)))))
        out = dot16(
            jnp.concatenate(left, axis=0), jnp.concatenate(right, axis=0), ((0,), (0,))
        )
        return out[:params], lanes_total(buf, depth, everyone)[:, 0:1]

    image1 = image_tangent(gathered(f1_recv, 0, depth))
    cotangent(image1, b1_send)
    to_owners(b1_send, b1_recv, 2)

    if views > 1:
        landed(xbuf, views - 1, 0)
    for k in range(1, views):
        other = lax.rem(my_view + k, views)
        onehot[other] = place_matrix(
            [xbuf[other, FEATS + b : FEATS + 1 + b, :] for b in range(blocks)]
        )

    landed(b1_recv, everyone - 1, 2)
    product, energy = parameters(b1_recv)
    product = product + damped
    step1 = rr / (energy + rdr)
    residual = right - step1 * product
    put(f2_send, 0, swapped(pick(small_dot(proj, residual), mine)))
    sums = (
        jnp.where(lane == 0, total(residual * residual), 0.0)
        + jnp.where(lane == 1, total(damp * residual * residual), 0.0)
        + jnp.where(lane == 2, total(damped * residual), 0.0)
    )
    for t in range(tiles):
        f2_send[t, depth] = sums
    to_tiles(f2_send, f2_recv, 3)

    landed(f2_recv, tiles - 1, 3)
    sums = lanes_total(f2_recv, depth, tiles)
    rr1, sds, sdr = sums[:, 0:1], sums[:, 1:2], sums[:, 2:3]
    beta = rr1 / rr
    image2 = image_tangent(gathered(f2_recv, 0, 0)) + beta * image1
    cotangent(image2, b2_send)
    to_owners(b2_send, b2_recv, 4)

    direction = residual + beta * right
    landed(b2_recv, everyone - 1, 4)
    product, energy = parameters(b2_recv)
    product = product + damp * direction
    step2 = rr1 / (energy + sds + 2.0 * beta * sdr + beta * beta * rdr)
    sol_ref[...] = step1 * right + step2 * direction
    res_ref[...] = residual - step2 * product

    if views > 1:
        left(xbuf, views - 1, 0)
    left(f1_recv, tiles - 1, 1)
    left(b1_recv, everyone - 1, 2)
    left(f2_recv, tiles - 1, 3)
    left(b2_recv, everyone - 1, 4)


def store(a_ref, b_ref, a_out, b_out, a_held, b_held, sem):
    rows = a_ref.shape[0]
    half = rows // 16 * 8
    parts = []
    for src, mid, out in ((a_ref, a_held, a_out), (b_ref, b_held, b_out)):
        for place in (pl.ds(0, half), pl.ds(half, rows - half)):
            number = len(parts)
            parts.append(
                (
                    pltpu.make_async_copy(src.at[place], mid.at[place], sem.at[0, number]),
                    pltpu.make_async_copy(mid.at[place], out.at[place], sem.at[1, number]),
                )
            )
    for come, go in parts:
        come.start()
    for come, go in parts:
        come.wait()
        go.start()
    for come, go in parts:
        go.wait()


def solution(mesh):
    views, tiles = mesh.shape["views"], mesh.shape["tiles"]

    def body(*args):
        linear_point, right_side, damping, proj, basis, weight, order, dest, depths = args
        gauss, count = order.shape[2], dest.shape[1]
        capacity = max(2, count // tiles)
        width = gauss // count * capacity
        depth = FEATS * width // 128
        args = (
            linear_point,
            right_side,
            damping,
            jnp.swapaxes(proj[0], 0, 1),
            jnp.swapaxes(basis[0], 0, 1),
            weight[0],
            order[0],
            dest.reshape(1, count),
            depths,
        )
        shape = jax.ShapeDtypeStruct(linear_point.shape, F32)
        vmem = pl.BlockSpec(memory_space=pltpu.VMEM)
        first, later = 2 * depth + 1, depth + 1
        results = pl.pallas_call(
            functools.partial(kernel, views, tiles),
            out_shape=(shape, shape),
            in_specs=[pl.BlockSpec(memory_space=pltpu.HBM)] * 9,
            out_specs=(vmem, vmem),
            scratch_shapes=[
                pltpu.VMEM((views, gauss, tiles * width), BF16),
                pltpu.VMEM((views, FEATS + 8, 128), F32),
                pltpu.VMEM((tiles, first, 1, 128), F32),
                pltpu.VMEM((tiles, first, 1, 128), F32),
                pltpu.VMEM((tiles, later, 1, 128), F32),
                pltpu.VMEM((views * tiles, later, 1, 128), F32),
                pltpu.VMEM((tiles, later, 1, 128), F32),
                pltpu.VMEM((tiles, later, 1, 128), F32),
                pltpu.VMEM((tiles, later, 1, 128), F32),
                pltpu.VMEM((views * tiles, later, 1, 128), F32),
            ]
            + [pltpu.VMEM(arg.shape, arg.dtype) for arg in args]
            + [
                pltpu.SemaphoreType.DMA((5,)),
                pltpu.SemaphoreType.DMA((5,)),
                pltpu.SemaphoreType.DMA((9,)),
            ],
            compiler_params=pltpu.CompilerParams(
                collective_id=0, has_side_effects=True, vmem_limit_bytes=63 * 1024 * 1024
            ),
        )(*args)
        return pl.pallas_call(
            store,
            out_shape=(shape, shape),
            in_specs=[pl.BlockSpec(memory_space=pltpu.HBM)] * 2,
            out_specs=(pl.BlockSpec(memory_space=pltpu.HBM),) * 2,
            scratch_shapes=[
                pltpu.VMEM(shape.shape, F32),
                pltpu.VMEM(shape.shape, F32),
                pltpu.SemaphoreType.DMA((2, 4)),
            ],
            compiler_params=pltpu.CompilerParams(vmem_limit_bytes=63 * 1024 * 1024),
        )(*results)

    in_specs = (
        P(None, "tiles"),
        P(None, "tiles"),
        P(None, "tiles"),
        P("views", None, None),
        P("views", "tiles", None, None),
        P("views", "tiles", None),
        P("views", "tiles", None),
        P("views", "tiles", None),
        P("views", "tiles"),
    )
    out_specs = (P(None, "tiles"), P(None, "tiles"))
    return jax.shard_map(body, mesh=mesh, in_specs=in_specs, out_specs=out_specs, check_vma=False)
```
